32 devices in a mesh: groups: 2 (over x), tm: 16 (over z, y, core).
Axes of the slice: x: 2, y: 2, z: 4, core: 2. Of those that a mesh axis runs over, the one named last changes fastest.
Arguments:
- latent: bfloat16 [64, 8192], P('groups', 'tm'), parts along dimension 0, may hold values from -6 to 6
- w_in: bfloat16 [3, 3, 3, 16, 384], replicated, may hold values from -0.3125 to 0.3125
- b_in: float32 [384], replicated, may hold values from -3 to 3
- gain: float32 [384], replicated, may hold values from 0.1 to 1.9
- w_mid: bfloat16 [3, 3, 3, 384, 384], replicated, may hold values from -0.0625 to 0.0625
- b_mid: float32 [384], replicated, may hold values from -3 to 3
- w_time: bfloat16 [3, 384, 768], replicated, may hold values from -0.1875 to 0.1875
- b_time: float32 [768], replicated, may hold values from -3 to 3
Outputs:
- frames_up: bfloat16 [128, 16, 32, 384], P(('groups', 'tm')), parts along dimension 0
The draws below stay inside these ranges and needn't reach their ends.
There are 2 independent parts, one for each index of `groups`. The reference program is written for one: setup_inputs(seed, part) draws one part's arguments, and reference() takes and returns one part's arrays. A program takes and returns all parts, laid end to end along the dimension named above; an argument that names none is the same for every part. Nothing has to cross between parts.
All inputs are finite; a program needn't handle non-finite values.
Results may differ from the reference program's by a relative error of at most 0.012.
Values may be sent and summed in bfloat16 or wider, within the bound.
No kernel may reach another device: no remote copies, remote signals or barrier semaphores. Data moves between devices by JAX's collectives and lax.ppermute only.
A program may use at most 128 MiB of HBM per device.

```python
import jax
import jax.numpy as jnp
from jax import lax

ZC = 16
C = 384
H = 16
W = 32
LF = 32


def shard_levels(key, dims, shards, low, high):
    factor_of, own = 1.0, jax.random.fold_in(key, 6)
    for position, shards_of in shards:
        steps = jnp.exp(jax.random.uniform(jax.random.fold_in(own, position), (shards_of,), jnp.float32, low / len(shards), high / len(shards)))
        factor_of = factor_of * jnp.repeat(steps, dims[position] // shards_of).reshape([-1 if axis == position else 1 for axis in range(len(dims))])
    return factor_of


def noise(rng, dims, scale, bound, split=(), held_as=jnp.bfloat16):
    entries = scale * jax.random.normal(rng, dims, jnp.float32)
    if split:
        entries = entries * shard_levels(rng, dims, split, -0.22, 0.18)
    return jnp.clip(entries, -bound, bound).astype(held_as)


def setup_inputs(seed: int = 0, part: int = 0) -> dict:
    streams_of = jax.random.split(jax.random.key(seed), 9)
    part_splits = jax.random.split(jax.random.fold_in(streams_of[8], part), 9)
    return {
        "latent": noise(part_splits[0], (LF, H * W * ZC), 1.0, 6.0, ((1, 16),)),
        "w_in": noise(streams_of[1], (3, 3, 3, ZC, C), (27 * ZC) ** -0.5, 0.3125),
        "b_in": noise(streams_of[2], (C,), 0.5, 3.0, (), jnp.float32),
        "gain": jnp.clip(1.0 + 0.18 * jax.random.normal(streams_of[3], (C,), jnp.float32), 0.1, 1.9),
        "w_mid": noise(streams_of[4], (3, 3, 3, C, C), (27 * C) ** -0.5, 0.0625),
        "b_mid": noise(streams_of[5], (C,), 0.5, 3.0, (), jnp.float32),
        "w_time": noise(streams_of[6], (3, C, 2 * C), (3 * C) ** -0.5, 0.1875),
        "b_time": noise(streams_of[7], (2 * C,), 0.5, 3.0, (), jnp.float32),
    }


def conv_valid(padded, weight, bias, spatial, edged):
    frames = padded.shape[0] - 2
    rows = padded.shape[1]
    inner = padded.shape[3]
    if spatial:
        margin = 0 if edged else 1
        padded = jnp.pad(padded, ((0, 0), (1, 1), (margin, margin), (0, 0)))
        taps = 3
    else:
        taps = 1
    cols = padded.shape[2] - taps + 1
    total = jnp.zeros((frames * rows * cols, weight.shape[-1]), jnp.float32)
    for step_t in range(3):
        for step_h in range(taps):
            for step_w in range(taps):
                window = padded[step_t:step_t + frames, step_h:step_h + rows, step_w:step_w + cols, :]
                if spatial:
                    kernel = weight[step_t, step_h, step_w]
                else:
                    kernel = weight[step_t]
                total = total + jnp.dot(window.reshape(-1, inner), kernel, preferred_element_type=jnp.float32)
    return (total + bias).reshape(frames, rows, cols, weight.shape[-1])

def conv_input(padded, weight, bias, edged):
    frames = padded.shape[0] - 2
    rows = padded.shape[1]
    inner = padded.shape[3]
    margin = 0 if edged else 1
    padded = jnp.pad(padded, ((0, 0), (1, 1), (margin, margin), (0, 0)))
    cols = padded.shape[2] - 2
    windows = []
    for step_t in range(3):
        for step_h in range(3):
            for step_w in range(3):
                windows.append(padded[step_t:step_t + frames, step_h:step_h + rows, step_w:step_w + cols, :])
    stacked = jnp.concatenate(windows, axis=-1).reshape(frames * rows * cols, 27 * inner)
    total = jnp.dot(stacked, weight.reshape(27 * inner, weight.shape[-1]), preferred_element_type=jnp.float32)
    return (total + bias).reshape(frames, rows, cols, weight.shape[-1])

def activate(hidden, gain):
    values = hidden.astype(jnp.float32)
    scale = jax.lax.rsqrt(lax.optimization_barrier(jnp.mean(values * values, axis=-1, keepdims=True)) + 1e-06)
    return jax.nn.silu(values * scale * gain).astype(jnp.bfloat16)

def reference(latent, w_in, b_in, gain, w_mid, b_mid, w_time, b_time):
    lat = latent.reshape(LF, H, W, ZC)
    zeros_in = jnp.zeros((2, H, W, ZC), latent.dtype)
    h0 = conv_input(jnp.concatenate([zeros_in, lat], axis=0), w_in, b_in, False).astype(jnp.bfloat16)
    act = activate(h0, gain)
    zeros_mid = jnp.zeros((2, H, W, C), jnp.bfloat16)
    h1 = (h0.astype(jnp.float32) + conv_valid(jnp.concatenate([zeros_mid, act], axis=0), w_mid, b_mid, True, False)).astype(jnp.bfloat16)
    up = conv_valid(jnp.concatenate([zeros_mid, h1], axis=0), w_time, b_time, False, False)
    paired = up.reshape(LF, H, W, 2, C).transpose(0, 3, 1, 2, 4)
    return paired.reshape(2 * LF, H, W, C).astype(jnp.bfloat16)
```

```python
import jax
import jax.numpy as jnp
from jax import lax
from jax.experimental import pallas as pl
from jax.experimental.pallas import tpu as pltpu
from jax.sharding import PartitionSpec as P

ZC = 16
C = 384
H = 16
W = 32
NT = 2
LATF = NT + 6
ACTF = NT + 4
MIDF = NT + 2
PAIRS = W // 2
LANES = 640
K3 = 3 * C
F32 = jnp.float32
BF16 = jnp.bfloat16


def kernel(
    x_ref, win_ref, bin_ref, gain_ref, wm_hbm, bmid_ref, wt_hbm, btime_ref, out_ref,
    wm, wt, toep, lhs, h0_s, vt, v_s, u_s, m_s, y_s, tr, hcat, sem_m, sem_t,
):
    copy_m = pltpu.make_async_copy(wm_hbm, wm, sem_m)
    copy_t = pltpu.make_async_copy(wt_hbm, wt, sem_t)
    copy_m.start()
    copy_t.start()
    first = lax.axis_index("tm") * NT

    toep[...] = jnp.zeros_like(toep)
    for dt in range(3):
        for dh in range(3):
            base = dt * 128 + dh * 64 if dh < 2 else 384 + dt * 128
            for j in range(4):
                for o in range(2):
                    dw = j - o
                    if 0 <= dw <= 2:
                        tap = ((dt * 3 + dh) * 3 + dw) * ZC
                        toep[base + 16 * j : base + 16 * j + 16, o * C : (o + 1) * C] = win_ref[
                            tap : tap + ZC, :
                        ]

    x = x_ref[...].astype(F32)
    row = lax.broadcasted_iota(jnp.int32, x.shape, 0) % H
    lane = lax.broadcasted_iota(jnp.int32, x.shape, 1) % 128
    above = jnp.where(row == 0, 0.0, pltpu.roll(x, 1, 0))
    below = jnp.where(row == H - 1, 0.0, pltpu.roll(x, x.shape[0] - 1, 0))
    for q in range(4):
        left = (LANES - 32 * q) % LANES
        mid = (LANES + 64 - 32 * q) % LANES
        a0 = pltpu.roll(above, left, 1) if left else above
        a1 = pltpu.roll(x, mid, 1) if mid else x
        a2 = pltpu.roll(below, left, 1) if left else below
        pair = jnp.where(lane < 64, a0, a1).astype(BF16)
        last = a2.astype(BF16)
        for g in range(4):
            for dt in range(3):
                rows = slice(g * ACTF * H, (g + 1) * ACTF * H)
                src = slice(dt * H, dt * H + ACTF * H)
                lhs[q, rows, dt * 128 : dt * 128 + 128] = pair[src, g * 128 : (g + 1) * 128]
                lhs[q, rows, 384 + dt * 128 : 512 + dt * 128] = last[src, g * 128 : (g + 1) * 128]

    for kt in range(4):
        for t in range(2):
            vt[kt, 0, t, 0] = jnp.zeros((H, K3), BF16)
            vt[kt, 1, t, PAIRS] = jnp.zeros((H, K3), BF16)
    b_in = bin_ref[...].reshape(1, C)
    gain = gain_ref[...].reshape(1, C)
    sub = lax.broadcasted_iota(jnp.int32, (8, C), 0)
    keep = [jnp.where(first - 4 + f >= 0, 1.0, 0.0).astype(F32) for f in range(ACTF)]

    @pl.loop(0, 4)
    def _(q):
        y = jnp.dot(lhs[q], toep[...], preferred_element_type=F32)
        for o in range(2):
            for g in range(4):
                part = y[g * ACTF * H : (g + 1) * ACTF * H, o * C : (o + 1) * C] + b_in
                hb = part.astype(BF16)
                for f in range(2, ACTF):
                    h0_s[f - 2, o, 4 * g + q] = hb[f * H : (f + 1) * H]
                h = hb.astype(F32)
                scale = lax.rsqrt(jnp.mean(h * h, axis=-1, keepdims=True) + 1e-06)
                v = h * scale * gain
                a = 0.5 * v * (1.0 + jnp.tanh(0.5 * v))
                d = [a[f * H : (f + 1) * H] * keep[f] for f in range(ACTF)]
                for t in range(2):
                    d0, d1, d2, d3 = d[2 * t : 2 * t + 4]
                    for kt, r in enumerate((d0 - d2, 0.5 * (d1 + d2), 0.5 * (d2 - d1), d1 - d3)):
                        lo, hi = r[:8], r[8:]
                        lo1, hi1 = pltpu.roll(lo, 1, 0), pltpu.roll(hi, 1, 0)
                        lo7, hi7 = pltpu.roll(lo, 7, 0), pltpu.roll(hi, 7, 0)
                        up = jnp.concatenate(
                            [jnp.where(sub == 0, 0.0, lo1), jnp.where(sub == 0, lo1, hi1)], axis=0
                        )
                        dn = jnp.concatenate(
                            [jnp.where(sub == 7, hi7, lo7), jnp.where(sub == 7, 0.0, hi7)], axis=0
                        )
                        at = vt.at[kt, 1 - o, t, 4 * g + q + o]
                        at[:, :C] = up.astype(BF16)
                        at[:, C : 2 * C] = r.astype(BF16)
                        at[:, 2 * C :] = dn.astype(BF16)

    copy_m.wait()
    for kt in range(4):

        @pl.loop(0, 3)
        def _(dh):
            @pl.loop(0, C // 16)
            def _(i):
                def tap(dt, dw):
                    at = ((dt * 3 + dh) * 3 + dw) * C + i * 16
                    return wm[pl.ds(pl.multiple_of(at, 16), 16), :]

                g = []
                for dw in range(3):
                    if kt == 0:
                        g.append(tap(0, dw))
                    elif kt == 3:
                        g.append(tap(2, dw))
                    elif kt == 1:
                        g.append((tap(0, dw) + tap(2, dw)) + tap(1, dw))
                    else:
                        g.append((tap(0, dw) + tap(2, dw)) - tap(1, dw))
                e = g[0] + g[2]
                rows = pl.ds(pl.multiple_of(dh * C + i * 16, 16), 16)
                for kc, u in enumerate((g[0], e + g[1], e - g[1], g[2])):
                    u_s[kc, rows, :] = u

        for t in range(2):

            @pl.loop(0, PAIRS)
            def _(ct):
                d0, d1 = vt[kt, 0, t, ct], vt[kt, 1, t, ct]
                d2, d3 = vt[kt, 0, t, ct + 1], vt[kt, 1, t, ct + 1]
                rows = pl.ds(pl.multiple_of((t * PAIRS + ct) * H, H), H)
                for kc, r in enumerate((d0 - d2, d1 + d2, d2 - d1, d1 - d3)):
                    v_s[kc, rows, :] = r

        for kc in range(4):
            m_s[kc] = jnp.dot(v_s[kc], u_s[kc], preferred_element_type=F32)

        @pl.loop(0, 2 * PAIRS)
        def _(i):
            rows = pl.ds(pl.multiple_of(i * H, H), H)
            m0, m1, m2, m3 = (m_s[kc, rows, :] for kc in range(4))
            y_s[kt, 0, rows, :] = m0 + 0.5 * (m1 + m2)
            y_s[kt, 1, rows, :] = 0.5 * (m1 - m2) - m3

    b_mid = bmid_ref[...].reshape(1, C)
    b_time = btime_ref[...].reshape(1, 2 * C)
    for t in range(2):

        @pl.loop(0, PAIRS)
        def _(ct):
            rows = pl.ds(pl.multiple_of((t * PAIRS + ct) * H, H), H)
            for o in range(2):
                y0, y1, y2, y3 = (y_s[kt, o, rows, :] for kt in range(4))
                for s, z in enumerate((y0 + (y1 + y2), (y1 - y2) - y3)):
                    f = 2 * t + s
                    h1 = h0_s[f, o, ct].astype(F32) + (z + b_mid)
                    h1 = h1 * jnp.where(first - 2 + f >= 0, 1.0, 0.0).astype(F32)
                    for k in range(3):
                        tr[f, k, pl.ds(2 * ct + o, H, stride=W), :] = h1[
                            :, k * 128 : (k + 1) * 128
                        ]

    for f in range(MIDF):
        for k in range(3):
            hcat[:, f * C + k * 128 : f * C + (k + 1) * 128] = tr[f, k].astype(BF16)
    copy_t.wait()
    for f in range(NT):
        up = jnp.dot(hcat[:, f * C : f * C + K3], wt[...], preferred_element_type=F32) + b_time
        for s in range(2):
            out_ref[2 * f + s] = up[:, s * C : (s + 1) * C].astype(BF16)


def per_device(latent, w_in, b_in, gain, w_mid, b_mid, w_time, b_time):
    n = lax.axis_size("tm")
    frames, width = latent.shape
    padded = jnp.concatenate([jnp.zeros((6, width), BF16), latent], axis=0)
    sent = jnp.concatenate(
        [padded[k : k + frames].reshape(n, NT, width) for k in range(0, LATF, NT)], axis=1
    )
    got = lax.all_to_all(sent, "tm", split_axis=0, concat_axis=0, tiled=True)
    x = got.transpose(1, 0, 2).reshape(LATF * H, W * ZC)
    x = jnp.pad(x, ((0, 0), (ZC, LANES - W * ZC - ZC)))
    vmem = pl.BlockSpec(memory_space=pltpu.VMEM)
    hbm = pl.BlockSpec(memory_space=pl.ANY)
    out = pl.pallas_call(
        kernel,
        out_shape=jax.ShapeDtypeStruct((2 * NT, H * W, C), BF16),
        in_specs=[vmem, vmem, vmem, vmem, hbm, vmem, hbm, vmem],
        out_specs=vmem,
        scratch_shapes=[
            pltpu.VMEM((27 * C, C), BF16),
            pltpu.VMEM((K3, 2 * C), BF16),
            pltpu.VMEM((2 * C, 2 * C), BF16),
            pltpu.VMEM((4, 4 * ACTF * H, 2 * C), BF16),
            pltpu.VMEM((MIDF, 2, PAIRS, H, C), BF16),
            pltpu.VMEM((4, 2, 2, PAIRS + 1, H, K3), BF16),
            pltpu.VMEM((4, 2 * PAIRS * H, K3), BF16),
            pltpu.VMEM((4, K3, C), BF16),
            pltpu.VMEM((4, H * W, C), F32),
            pltpu.VMEM((4, 2, 2 * PAIRS * H, C), F32),
            pltpu.VMEM((MIDF, 3, H * W, 128), F32),
            pltpu.VMEM((H * W, MIDF * C), BF16),
            pltpu.SemaphoreType.DMA,
            pltpu.SemaphoreType.DMA,
        ],
        compiler_params=pltpu.CompilerParams(vmem_limit_bytes=60 * 2**20),
    )(
        x, w_in.reshape(27 * ZC, C), b_in, gain, w_mid.reshape(27 * C, C), b_mid,
        w_time.reshape(K3, 2 * C), b_time,
    )
    return out.reshape(2 * NT, H, W, C)


def solution(mesh):
    return jax.shard_map(
        per_device,
        mesh=mesh,
        in_specs=(P("groups", "tm"), P(), P(), P(), P(), P(), P(), P()),
        out_specs=P(("groups", "tm"), None, None, None),
        check_vma=False,
    )
```

```python
import jax
import jax.numpy as jnp
from jax import lax
from jax.experimental import pallas as pl
from jax.experimental.pallas import tpu as pltpu
from jax.sharding import PartitionSpec as P

ZC = 16
C = 384
H = 16
W = 32
NT = 2
LATF = NT + 6
ACTF = NT + 4
MIDF = NT + 2
PAIRS = W // 2
LANES = 640
K3 = 3 * C
BLOCK = 4 * ACTF * H
EIGHTH = C // 8
F32 = jnp.float32
BF16 = jnp.bfloat16


def kernel(
    x_ref, win_ref, bin_ref, gain_ref, wm_hbm, bmid_ref, wt_hbm, btime_ref, out_ref,
    wm, wt, toep, lhs, h0_s, vt, v_s, u_s, m_s, y_s, hcat, perm, sem_m, sem_t,
):
    copy_m = pltpu.make_async_copy(wm_hbm, wm, sem_m)
    copy_t = pltpu.make_async_copy(wt_hbm, wt, sem_t)
    copy_m.start()
    copy_t.start()
    first = lax.axis_index("tm") * NT

    to = lax.broadcasted_iota(jnp.int32, perm.shape, 0)
    of = lax.broadcasted_iota(jnp.int32, perm.shape, 1)
    source = (to % 2) * (PAIRS * H) + (to % W) // 2 * H + to // W
    perm[...] = jnp.where(source == of, 1.0, 0.0).astype(BF16)

    toep[...] = jnp.zeros_like(toep)
    for dt in range(3):
        for dh in range(3):
            base = dt * 128 + dh * 64 if dh < 2 else 384 + dt * 128
            for j in range(4):
                for o in range(2):
                    dw = j - o
                    if 0 <= dw <= 2:
                        tap = ((dt * 3 + dh) * 3 + dw) * ZC
                        toep[base + 16 * j : base + 16 * j + 16, o * C : (o + 1) * C] = win_ref[
                            tap : tap + ZC, :
                        ]

    x = x_ref[...].astype(F32)
    row = lax.broadcasted_iota(jnp.int32, x.shape, 0) % H
    lane = lax.broadcasted_iota(jnp.int32, x.shape, 1) % 128
    above = jnp.where(row == 0, 0.0, pltpu.roll(x, 1, 0))
    below = jnp.where(row == H - 1, 0.0, pltpu.roll(x, x.shape[0] - 1, 0))
    for q in range(4):
        left = (LANES - 32 * q) % LANES
        mid = (LANES + 64 - 32 * q) % LANES
        a0 = pltpu.roll(above, left, 1) if left else above
        a1 = pltpu.roll(x, mid, 1) if mid else x
        a2 = pltpu.roll(below, left, 1) if left else below
        pair = jnp.where(lane < 64, a0, a1).astype(BF16)
        last = a2.astype(BF16)
        for g in range(4):
            for dt in range(3):
                rows = slice(q * BLOCK + g * ACTF * H, q * BLOCK + (g + 1) * ACTF * H)
                src = slice(dt * H, dt * H + ACTF * H)
                lhs[rows, dt * 128 : dt * 128 + 128] = pair[src, g * 128 : (g + 1) * 128]
                lhs[rows, 384 + dt * 128 : 512 + dt * 128] = last[src, g * 128 : (g + 1) * 128]

    for kt in range(4):
        for t in range(2):
            vt[kt, 0, t, 0] = jnp.zeros((H, K3), BF16)
            vt[kt, 1, t, PAIRS] = jnp.zeros((H, K3), BF16)
    b_in = bin_ref[...].reshape(1, C)
    gain = gain_ref[...].reshape(1, C)
    sub = lax.broadcasted_iota(jnp.int32, (8, C), 0)
    keep = [jnp.where(first - 4 + f >= 0, 1.0, 0.0).astype(F32) for f in range(ACTF)]

    def conv_in(q, slot):
        rows = pl.ds(pl.multiple_of(q * BLOCK, BLOCK), BLOCK)
        y = jnp.dot(lhs[rows, :], toep[...], preferred_element_type=F32)
        for o in range(2):
            m_s[slot, o, :BLOCK, :] = y[:, o * C : (o + 1) * C]

    def activate(q, slot):
        for o in range(2):
            for g in range(4):
                part = m_s[slot, o, g * ACTF * H : (g + 1) * ACTF * H, :] + b_in
                hb = part.astype(BF16)
                for f in range(2, ACTF):
                    h0_s[f - 2, o, 4 * g + q] = hb[f * H : (f + 1) * H]
                h = hb.astype(F32)
                scale = lax.rsqrt(jnp.mean(h * h, axis=-1, keepdims=True) + 1e-06)
                v = h * scale * gain
                a = 0.5 * v * (1.0 + jnp.tanh(0.5 * v))
                d = [a[f * H : (f + 1) * H] * keep[f] for f in range(ACTF)]
                for t in range(2):
                    d0, d1, d2, d3 = d[2 * t : 2 * t + 4]
                    for kt, r in enumerate((d0 - d2, 0.5 * (d1 + d2), 0.5 * (d2 - d1), d1 - d3)):
                        lo, hi = r[:8], r[8:]
                        lo1, hi1 = pltpu.roll(lo, 1, 0), pltpu.roll(hi, 1, 0)
                        lo7, hi7 = pltpu.roll(lo, 7, 0), pltpu.roll(hi, 7, 0)
                        up = jnp.concatenate(
                            [jnp.where(sub == 0, 0.0, lo1), jnp.where(sub == 0, lo1, hi1)], axis=0
                        )
                        dn = jnp.concatenate(
                            [jnp.where(sub == 7, hi7, lo7), jnp.where(sub == 7, 0.0, hi7)], axis=0
                        )
                        at = vt.at[kt, 1 - o, t, 4 * g + q + o]
                        at[:, :C] = up.astype(BF16)
                        at[:, C : 2 * C] = r.astype(BF16)
                        at[:, 2 * C :] = dn.astype(BF16)

    conv_in(0, 0)

    @pl.loop(0, 3)
    def _(q):
        conv_in(q + 1, (q + 1) % 2)
        activate(q, q % 2)

    activate(3, 1)
    copy_m.wait()

    def weights(kt, j):
        slot = kt % 2
        for dh in range(3):
            for i in range(EIGHTH // 16):

                def tap(dt, dw):
                    at = ((dt * 3 + dh) * 3 + dw) * C + j * EIGHTH + i * 16
                    return wm[pl.ds(at, 16), :]

                g = []
                for dw in range(3):
                    if kt == 0:
                        g.append(tap(0, dw))
                    elif kt == 3:
                        g.append(tap(2, dw))
                    elif kt == 1:
                        g.append((tap(0, dw) + tap(2, dw)) + tap(1, dw))
                    else:
                        g.append((tap(0, dw) + tap(2, dw)) - tap(1, dw))
                e = g[0] + g[2]
                rows = pl.ds(dh * C + j * EIGHTH + i * 16, 16)
                for kc, u in enumerate((g[0], e + g[1], e - g[1], g[2])):
                    u_s[slot, kc, rows, :] = u

    def columns(kt, j):
        slot = kt % 2
        for i in range(4):
            t, ct = j // 4, (j % 4) * 4 + i
            d0, d1 = vt[kt, 0, t, ct], vt[kt, 1, t, ct]
            d2, d3 = vt[kt, 0, t, ct + 1], vt[kt, 1, t, ct + 1]
            rows = pl.ds((j * 4 + i) * H, H)
            for kc, r in enumerate((d0 - d2, d1 + d2, d2 - d1, d1 - d3)):
                v_s[slot, kc, rows, :] = r

    def product(kt, j):
        slot = kt % 2
        kc = j // 2
        rows = pl.ds(j % 2 * 256, 256)
        m_s[slot, kc, rows, :] = jnp.dot(
            v_s[slot, kc, rows, :], u_s[slot, kc], preferred_element_type=F32
        )

    def inverse(kt, rows):
        m0, m1, m2, m3 = (m_s[kt % 2, kc, rows, :] for kc in range(4))
        return m0 + 0.5 * (m1 + m2), 0.5 * (m1 - m2) - m3

    for j in range(8):
        weights(0, j)
        columns(0, j)

    for kt in range(4):
        for j in range(8):
            product(kt, j)
            if kt < 3:
                weights(kt + 1, j)
                columns(kt + 1, j)
            if kt > 0:
                for i in range(4):
                    rows = pl.ds((j * 4 + i) * H, H)
                    y_s[kt - 1, 0, rows, :], y_s[kt - 1, 1, rows, :] = inverse(kt - 1, rows)

    b_mid = bmid_ref[...].reshape(1, C)
    b_time = btime_ref[...].reshape(1, 2 * C)
    for t in range(2):

        @pl.loop(0, PAIRS)
        def _(ct):
            rows = pl.ds(pl.multiple_of((t * PAIRS + ct) * H, H), H)
            y3s = inverse(3, rows)
            for o in range(2):
                y0, y1, y2 = (y_s[kt, o, rows, :] for kt in range(3))
                y3 = y3s[o]
                for s, z in enumerate((y0 + (y1 + y2), (y1 - y2) - y3)):
                    h1 = h0_s[2 * t + s, o, ct].astype(F32) + (z + b_mid)
                    h1 = h1 * jnp.where(first - 2 + 2 * t + s >= 0, 1.0, 0.0).astype(F32)
                    at = pl.ds(pl.multiple_of(t * H * W + o * PAIRS * H + ct * H, H), H)
                    lhs[at, s * C : (s + 1) * C] = h1.astype(BF16)

    for t in range(2):
        hcat[:, 2 * t * C : 2 * (t + 1) * C] = jnp.dot(
            perm[...], lhs[t * H * W : (t + 1) * H * W, :], preferred_element_type=F32
        ).astype(BF16)
    copy_t.wait()
    for f in range(NT):
        up = jnp.dot(hcat[:, f * C : f * C + K3], wt[...], preferred_element_type=F32) + b_time
        for s in range(2):
            out_ref[2 * f + s] = up[:, s * C : (s + 1) * C].astype(BF16)


def per_device(latent, w_in, b_in, gain, w_mid, b_mid, w_time, b_time):
    n = lax.axis_size("tm")
    frames, width = latent.shape
    padded = jnp.concatenate([jnp.zeros((6, width), BF16), latent], axis=0)
    sent = jnp.concatenate(
        [padded[k : k + frames].reshape(n, NT, width) for k in range(0, LATF, NT)], axis=1
    )
    got = lax.all_to_all(sent, "tm", split_axis=0, concat_axis=0, tiled=True)
    x = got.transpose(1, 0, 2).reshape(LATF * H, W * ZC)
    x = jnp.pad(x, ((0, 0), (ZC, LANES - W * ZC - ZC)))
    vmem = pl.BlockSpec(memory_space=pltpu.VMEM)
    hbm = pl.BlockSpec(memory_space=pl.ANY)
    out = pl.pallas_call(
        kernel,
        out_shape=jax.ShapeDtypeStruct((2 * NT, H * W, C), BF16),
        in_specs=[vmem, vmem, vmem, vmem, hbm, vmem, hbm, vmem],
        out_specs=vmem,
        scratch_shapes=[
            pltpu.VMEM((27 * C, C), BF16),
            pltpu.VMEM((K3, 2 * C), BF16),
            pltpu.VMEM((2 * C, 2 * C), BF16),
            pltpu.VMEM((4 * BLOCK, 2 * C), BF16),
            pltpu.VMEM((MIDF, 2, PAIRS, H, C), BF16),
            pltpu.VMEM((4, 2, 2, PAIRS + 1, H, K3), BF16),
            pltpu.VMEM((2, 4, 2 * PAIRS * H, K3), BF16),
            pltpu.VMEM((2, 4, K3, C), BF16),
            pltpu.VMEM((2, 4, H * W, C), F32),
            pltpu.VMEM((3, 2, 2 * PAIRS * H, C), F32),
            pltpu.VMEM((H * W, MIDF * C), BF16),
            pltpu.VMEM((H * W, H * W), BF16),
            pltpu.SemaphoreType.DMA,
            pltpu.SemaphoreType.DMA,
        ],
        compiler_params=pltpu.CompilerParams(vmem_limit_bytes=62 * 2**20),
    )(
        x, w_in.reshape(27 * ZC, C), b_in, gain, w_mid.reshape(27 * C, C), b_mid,
        w_time.reshape(K3, 2 * C), b_time,
    )
    return out.reshape(2 * NT, H, W, C)


def solution(mesh):
    return jax.shard_map(
        per_device,
        mesh=mesh,
        in_specs=(P("groups", "tm"), P(), P(), P(), P(), P(), P(), P()),
        out_specs=P(("groups", "tm"), None, None, None),
        check_vma=False,
    )
```

```python
import jax
import jax.numpy as jnp
from jax import lax
from jax.experimental import pallas as pl
from jax.experimental.pallas import tpu as pltpu
from jax.sharding import PartitionSpec as P

ZC = 16
C = 384
H = 16
W = 32
NT = 2
LATF = NT + 6
ACTF = NT + 4
MIDF = NT + 2
PAIRS = W // 2
LANES = 640
K3 = 3 * C
BLOCK = 4 * ACTF * H
EIGHTH = C // 8
F32 = jnp.float32
BF16 = jnp.bfloat16


def kernel(
    x_hbm, win_hbm, bin_ref, gain_ref, wm_hbm, bmid_ref, wt_hbm, btime_ref, out_hbm,
    x_s, win, wm, wt, toep, lhs, h0_s, vt, v_s, u_s, m_s, y_s, hcat, perm, out_s, sems, out_sems,
):
    copies = [
        pltpu.make_async_copy(src, dst, sems.at[i])
        for i, (src, dst) in enumerate(((x_hbm, x_s), (win_hbm, win), (wm_hbm, wm), (wt_hbm, wt)))
    ]
    for copy in copies:
        copy.start()
    copy_x, copy_in, copy_m, copy_t = copies
    first = lax.axis_index("tm") * NT

    to = lax.broadcasted_iota(jnp.int32, perm.shape, 0)
    of = lax.broadcasted_iota(jnp.int32, perm.shape, 1)
    source = (to % 2) * (PAIRS * H) + (to % W) // 2 * H + to // W
    perm[...] = jnp.where(source == of, 1.0, 0.0).astype(BF16)

    toep[...] = jnp.zeros_like(toep)
    copy_in.wait()
    for dt in range(3):
        for dh in range(3):
            base = dt * 128 + dh * 64 if dh < 2 else 384 + dt * 128
            for j in range(4):
                for o in range(2):
                    dw = j - o
                    if 0 <= dw <= 2:
                        tap = ((dt * 3 + dh) * 3 + dw) * ZC
                        toep[base + 16 * j : base + 16 * j + 16, o * C : (o + 1) * C] = win[
                            tap : tap + ZC, :
                        ]

    copy_x.wait()
    pieces = W * ZC // x_s.shape[1]
    to = lax.broadcasted_iota(jnp.int32, (LATF * H, x_s.shape[0]), 0)
    of = lax.broadcasted_iota(jnp.int32, (LATF * H, x_s.shape[0]), 1)
    x = [
        jnp.dot(
            jnp.where((to % H * pieces + i) * LATF + to // H == of, 1.0, 0.0).astype(BF16),
            x_s[...],
            preferred_element_type=F32,
        )
        for i in range(pieces)
    ]
    x = jnp.concatenate([*x, jnp.zeros((LATF * H, LANES - W * ZC), F32)], axis=1)
    x = pltpu.roll(x, ZC, 1)
    row = lax.broadcasted_iota(jnp.int32, x.shape, 0) % H
    lane = lax.broadcasted_iota(jnp.int32, x.shape, 1) % 128
    above = jnp.where(row == 0, 0.0, pltpu.roll(x, 1, 0))
    below = jnp.where(row == H - 1, 0.0, pltpu.roll(x, x.shape[0] - 1, 0))
    for q in range(4):
        left = (LANES - 32 * q) % LANES
        mid = (LANES + 64 - 32 * q) % LANES
        a0 = pltpu.roll(above, left, 1) if left else above
        a1 = pltpu.roll(x, mid, 1) if mid else x
        a2 = pltpu.roll(below, left, 1) if left else below
        pair = jnp.where(lane < 64, a0, a1).astype(BF16)
        last = a2.astype(BF16)
        for g in range(4):
            for dt in range(3):
                rows = slice(q * BLOCK + g * ACTF * H, q * BLOCK + (g + 1) * ACTF * H)
                src = slice(dt * H, dt * H + ACTF * H)
                lhs[rows, dt * 128 : dt * 128 + 128] = pair[src, g * 128 : (g + 1) * 128]
                lhs[rows, 384 + dt * 128 : 512 + dt * 128] = last[src, g * 128 : (g + 1) * 128]

    for kt in range(4):
        for t in range(2):
            vt[kt, 0, t, 0] = jnp.zeros((H, K3), BF16)
            vt[kt, 1, t, PAIRS] = jnp.zeros((H, K3), BF16)
    b_in = bin_ref[...].reshape(1, C)
    half_gain = 0.5 * gain_ref[...].reshape(1, C)
    sub = lax.broadcasted_iota(jnp.int32, (8, C), 0)
    frame = lax.broadcasted_iota(jnp.int32, (ACTF * H, 1), 0) // H + (first - 4)
    keep = jnp.where(frame >= 0, 1.0, 0.0).astype(F32)

    def conv_in(q, slot):
        rows = pl.ds(pl.multiple_of(q * BLOCK, BLOCK), BLOCK)
        y = jnp.dot(lhs[rows, :], toep[...], preferred_element_type=F32)
        for o in range(2):
            m_s[slot, o, :BLOCK, :] = y[:, o * C : (o + 1) * C]

    def activate(q, slot):
        for o in range(2):
            for g in range(4):
                part = m_s[slot, o, g * ACTF * H : (g + 1) * ACTF * H, :] + b_in
                hb = part.astype(BF16)
                for f in range(2, ACTF):
                    h0_s[f - 2, o, 4 * g + q] = hb[f * H : (f + 1) * H]
                h = hb.astype(F32)
                scale = lax.rsqrt(jnp.mean(h * h, axis=-1, keepdims=True) + 1e-06)
                v = h * (scale * keep) * half_gain
                a = v + v * jnp.tanh(v)
                d = [a[f * H : (f + 1) * H] for f in range(ACTF)]
                for t in range(2):
                    d0, d1, d2, d3 = d[2 * t : 2 * t + 4]
                    for kt, r in enumerate((d0 - d2, 0.5 * (d1 + d2), 0.5 * (d2 - d1), d1 - d3)):
                        lo, hi = r[:8], r[8:]
                        lo1, hi1 = pltpu.roll(lo, 1, 0), pltpu.roll(hi, 1, 0)
                        lo7, hi7 = pltpu.roll(lo, 7, 0), pltpu.roll(hi, 7, 0)
                        up = jnp.concatenate(
                            [jnp.where(sub == 0, 0.0, lo1), jnp.where(sub == 0, lo1, hi1)], axis=0
                        )
                        dn = jnp.concatenate(
                            [jnp.where(sub == 7, hi7, lo7), jnp.where(sub == 7, 0.0, hi7)], axis=0
                        )
                        at = vt.at[kt, 1 - o, t, 4 * g + q + o]
                        at[:, :C] = up.astype(BF16)
                        at[:, C : 2 * C] = r.astype(BF16)
                        at[:, 2 * C :] = dn.astype(BF16)

    conv_in(0, 0)

    @pl.loop(0, 3)
    def _(q):
        conv_in(q + 1, (q + 1) % 2)
        activate(q, q % 2)

    activate(3, 1)
    copy_m.wait()

    def weights(kt, j):
        slot = kt % 2
        for dh in range(3):
            for i in range(EIGHTH // 16):

                def tap(dt, dw):
                    at = ((dt * 3 + dh) * 3 + dw) * C + j * EIGHTH + i * 16
                    return wm[pl.ds(at, 16), :]

                g = []
                for dw in range(3):
                    if kt == 0:
                        g.append(tap(0, dw))
                    elif kt == 3:
                        g.append(tap(2, dw))
                    elif kt == 1:
                        g.append((tap(0, dw) + tap(2, dw)) + tap(1, dw))
                    else:
                        g.append((tap(0, dw) + tap(2, dw)) - tap(1, dw))
                e = g[0] + g[2]
                rows = pl.ds(dh * C + j * EIGHTH + i * 16, 16)
                for kc, u in enumerate((g[0], e + g[1], e - g[1], g[2])):
                    u_s[slot, kc, rows, :] = u

    def columns(kt, j):
        slot = kt % 2
        for i in range(4):
            t, ct = j // 4, (j % 4) * 4 + i
            d0, d1 = vt[kt, 0, t, ct], vt[kt, 1, t, ct]
            d2, d3 = vt[kt, 0, t, ct + 1], vt[kt, 1, t, ct + 1]
            rows = pl.ds((j * 4 + i) * H, H)
            for kc, r in enumerate((d0 - d2, d1 + d2, d2 - d1, d1 - d3)):
                v_s[slot, kc, rows, :] = r

    def product(kt, j):
        slot = kt % 2
        kc = j // 2
        rows = pl.ds(j % 2 * 256, 256)
        m_s[slot, kc, rows, :] = jnp.dot(
            v_s[slot, kc, rows, :], u_s[slot, kc], preferred_element_type=F32
        )

    def inverse(kt, rows):
        m0, m1, m2, m3 = (m_s[kt % 2, kc, rows, :] for kc in range(4))
        return m0 + 0.5 * (m1 + m2), 0.5 * (m1 - m2) - m3

    for j in range(8):
        weights(0, j)
        columns(0, j)

    for kt in range(4):
        for j in range(8):
            product(kt, j)
            if kt < 3:
                weights(kt + 1, j)
                columns(kt + 1, j)
            if kt > 0:
                for i in range(4):
                    rows = pl.ds((j * 4 + i) * H, H)
                    y_s[kt - 1, 0, rows, :], y_s[kt - 1, 1, rows, :] = inverse(kt - 1, rows)

    b_mid = bmid_ref[...].reshape(1, C)
    b_time = btime_ref[...].reshape(1, 2 * C)
    for t in range(2):
        for ct in range(PAIRS):
            rows = slice((t * PAIRS + ct) * H, (t * PAIRS + ct + 1) * H)
            y3s = inverse(3, rows)
            for o in range(2):
                y0, y1, y2 = (y_s[kt, o, rows, :] for kt in range(3))
                y3 = y3s[o]
                for s, z in enumerate((y0 + (y1 + y2), (y1 - y2) - y3)):
                    h1 = h0_s[2 * t + s, o, ct].astype(F32) + (z + b_mid)
                    if t == 0:
                        h1 = h1 * jnp.where(first - 2 + s >= 0, 1.0, 0.0).astype(F32)
                    at = t * H * W + o * PAIRS * H + ct * H
                    lhs[at : at + H, s * C : (s + 1) * C] = h1.astype(BF16)
        hcat[:, 2 * t * C : 2 * (t + 1) * C] = jnp.dot(
            perm[...], lhs[t * H * W : (t + 1) * H * W, :], preferred_element_type=F32
        ).astype(BF16)
    copy_t.wait()
    sent = []
    for f in range(NT):
        for part in range(2):
            rows = slice(part * H * W // 2, (part + 1) * H * W // 2)
            up = jnp.dot(hcat[rows, f * C : f * C + K3], wt[...], preferred_element_type=F32) + b_time
            for s in range(2):
                out_s[2 * f + s, rows, :] = up[:, s * C : (s + 1) * C].astype(BF16)
            here = (slice(2 * f, 2 * f + 2), rows)
            copy = pltpu.make_async_copy(out_s.at[here], out_hbm.at[here], out_sems.at[f, part])
            copy.start()
            sent.append(copy)
    for copy in sent:
        copy.wait()


def pack(latent_ref, out_ref, held):
    held[:LATF] = jnp.zeros_like(held[:LATF])
    held[LATF:] = latent_ref[...].astype(F32)
    for i in range(out_ref.shape[0]):
        out_ref[i] = held[NT * (i + 1) : NT * (i + 1) + LATF].astype(BF16)


def per_device(latent, w_in, b_in, gain, w_mid, b_mid, w_time, b_time):
    n = lax.axis_size("tm")
    frames, width = latent.shape
    sent = pl.pallas_call(
        pack,
        out_shape=jax.ShapeDtypeStruct((n, LATF, width), BF16),
        scratch_shapes=[pltpu.VMEM((LATF + frames, width), F32)],
    )(latent)
    x = lax.all_to_all(sent, "tm", split_axis=0, concat_axis=0, tiled=True)
    x = x.reshape(n * LATF, width)
    vmem = pl.BlockSpec(memory_space=pltpu.VMEM)
    hbm = pl.BlockSpec(memory_space=pl.ANY)
    out = pl.pallas_call(
        kernel,
        out_shape=jax.ShapeDtypeStruct((2 * NT, H * W, C), BF16),
        in_specs=[hbm, hbm, vmem, vmem, hbm, vmem, hbm, vmem],
        out_specs=hbm,
        scratch_shapes=[
            pltpu.VMEM((n * LATF, width), BF16),
            pltpu.VMEM((27 * ZC, C), BF16),
            pltpu.VMEM((27 * C, C), BF16),
            pltpu.VMEM((K3, 2 * C), BF16),
            pltpu.VMEM((2 * C, 2 * C), BF16),
            pltpu.VMEM((4 * BLOCK, 2 * C), BF16),
            pltpu.VMEM((MIDF, 2, PAIRS, H, C), BF16),
            pltpu.VMEM((4, 2, 2, PAIRS + 1, H, K3), BF16),
            pltpu.VMEM((2, 4, 2 * PAIRS * H, K3), BF16),
            pltpu.VMEM((2, 4, K3, C), BF16),
            pltpu.VMEM((2, 4, H * W, C), F32),
            pltpu.VMEM((3, 2, 2 * PAIRS * H, C), F32),
            pltpu.VMEM((H * W, MIDF * C), BF16),
            pltpu.VMEM((H * W, H * W), BF16),
            pltpu.VMEM((2 * NT, H * W, C), BF16),
            pltpu.SemaphoreType.DMA((4,)),
            pltpu.SemaphoreType.DMA((NT, 2)),
        ],
        compiler_params=pltpu.CompilerParams(vmem_limit_bytes=61 * 2**20),
    )(
        x, w_in.reshape(27 * ZC, C), b_in, gain, w_mid.reshape(27 * C, C), b_mid,
        w_time.reshape(K3, 2 * C), b_time,
    )
    return out.reshape(2 * NT, H, W, C)


def solution(mesh):
    return jax.shard_map(
        per_device,
        mesh=mesh,
        in_specs=(P("groups", "tm"), P(), P(), P(), P(), P(), P(), P()),
        out_specs=P(("groups", "tm"), None, None, None),
        check_vma=False,
    )
```

```python
import functools

import jax
import jax.numpy as jnp
from jax import lax
from jax.experimental import pallas as pl
from jax.experimental.pallas import tpu as pltpu
from jax.sharding import PartitionSpec as P

ZC = 16
C = 384
H = 16
W = 32
NT = 2
LATF = NT + 6
ACTF = NT + 4
MIDF = NT + 2
PAIRS = W // 2
LANES = 640
K3 = 3 * C
BLOCK = 4 * ACTF * H
POINTS = 6
ORDER = (0, 5, 1, 2, 3, 4)
QUARTER = C // 4
EIGHTH = C // 8
F32 = jnp.float32
BF16 = jnp.bfloat16


def time_points(d0, d1, d2, d3, d4, d5):
    p, q = d3 - d1, d4 - d2
    a, b = q + 1.5 * d3, p + 1.5 * d2
    first = (d0 - d2) + (q + 1.5 * p)
    last = (d5 - d3) + (1.5 * q - p)
    return first, a + b, a - b, 2.0 * p + q, 2.0 * q - p, last


def time_weights(kt, dw, tap):
    if kt == 0:
        return tap(0, dw)
    if kt == 5:
        return tap(2, dw)
    g0, g1, g2 = (tap(dt, dw) for dt in range(3))
    if kt == 1:
        return (g0 + g2) + g1
    if kt == 2:
        return (g0 + g2) - g1
    if kt == 3:
        return (4.0 * g0 + g2) + 2.0 * g1
    return (g0 + 4.0 * g2) - 2.0 * g1


def time_frames(m0, m1, m2, m3, m4, m5):
    s, d = (m1 - m2) * (1 / 3), (m1 + m2) * (1 / 3)
    a, b = m3 * (-4 / 15), m4 * (1 / 30)
    return (
        (m0 + s) + (a + b),
        d + (0.5 * a - 2.0 * b),
        s + (0.25 * a + 4.0 * b),
        (d + m5) + (0.125 * a - 8.0 * b),
    )


def kernel(
    x_hbm, win_hbm, bin_ref, gain_ref, wm_hbm, bmid_ref, wt_hbm, btime_ref, out_hbm,
    x_s, win, wm, wt, toep, lhs, h1_s, h0_s, vt, v_s, u_s, m_s, y_s, hcat, perm, sems, out_sems,
):
    copies = [
        pltpu.make_async_copy(src, dst, sems.at[i])
        for i, (src, dst) in enumerate(((x_hbm, x_s), (win_hbm, win), (wm_hbm, wm), (wt_hbm, wt)))
    ]
    for copy in copies:
        copy.start()
    copy_x, copy_in, copy_m, copy_t = copies
    first = lax.axis_index("tm") * NT

    to = lax.broadcasted_iota(jnp.int32, perm.shape, 0)
    of = lax.broadcasted_iota(jnp.int32, perm.shape, 1)
    source = (to % 2) * (PAIRS * H) + (to % W) // 2 * H + to // W
    perm[...] = jnp.where(source == of, 1.0, 0.0).astype(BF16)

    toep[...] = jnp.zeros_like(toep)
    copy_in.wait()
    for dt in range(3):
        for dh in range(3):
            base = dt * 128 + dh * 64 if dh < 2 else 384 + dt * 128
            for j in range(4):
                for o in range(2):
                    dw = j - o
                    if 0 <= dw <= 2:
                        tap = ((dt * 3 + dh) * 3 + dw) * ZC
                        toep[base + 16 * j : base + 16 * j + 16, o * C : (o + 1) * C] = win[
                            tap : tap + ZC, :
                        ]

    copy_x.wait()
    pieces = W * ZC // x_s.shape[1]
    to = lax.broadcasted_iota(jnp.int32, (LATF * H, x_s.shape[0]), 0)
    of = lax.broadcasted_iota(jnp.int32, (LATF * H, x_s.shape[0]), 1)
    x = [
        jnp.dot(
            jnp.where((to % H * pieces + i) * LATF + to // H == of, 1.0, 0.0).astype(BF16),
            x_s[...],
            preferred_element_type=F32,
        )
        for i in range(pieces)
    ]
    x = jnp.concatenate([*x, jnp.zeros((LATF * H, LANES - W * ZC), F32)], axis=1)
    x = pltpu.roll(x, ZC, 1)
    row = lax.broadcasted_iota(jnp.int32, x.shape, 0) % H
    lane = lax.broadcasted_iota(jnp.int32, x.shape, 1) % 128
    above = jnp.where(row == 0, 0.0, pltpu.roll(x, 1, 0))
    below = jnp.where(row == H - 1, 0.0, pltpu.roll(x, x.shape[0] - 1, 0))
    for q in range(4):
        left = (LANES - 32 * q) % LANES
        mid = (LANES + 64 - 32 * q) % LANES
        a0 = pltpu.roll(above, left, 1) if left else above
        a1 = pltpu.roll(x, mid, 1) if mid else x
        a2 = pltpu.roll(below, left, 1) if left else below
        pair = jnp.where(lane < 64, a0, a1).astype(BF16)
        last = a2.astype(BF16)
        for g in range(4):
            for dt in range(3):
                rows = slice(g * ACTF * H, (g + 1) * ACTF * H)
                src = slice(dt * H, dt * H + ACTF * H)
                lhs[q][rows, dt * 128 : dt * 128 + 128] = pair[src, g * 128 : (g + 1) * 128]
                lhs[q][rows, 384 + dt * 128 : 512 + dt * 128] = last[src, g * 128 : (g + 1) * 128]

    for kt in range(POINTS):
        vt[kt][0, 0] = jnp.zeros((H, K3), BF16)
        vt[kt][1, PAIRS] = jnp.zeros((H, K3), BF16)
    b_in = bin_ref[...].reshape(1, C)
    half_gain = 0.5 * gain_ref[...].reshape(1, C)
    sub = lax.broadcasted_iota(jnp.int32, (8, C), 0)
    frame = lax.broadcasted_iota(jnp.int32, (ACTF * H, 1), 0) // H + (first - 4)
    keep = jnp.where(frame >= 0, 1.0, 0.0).astype(F32)

    def conv_in(q):
        y = jnp.dot(lhs[q][...], toep[...], preferred_element_type=F32)
        for o in range(2):
            m_s[q % 2][o * BLOCK : (o + 1) * BLOCK, :] = y[:, o * C : (o + 1) * C]

    def activate(q):
        for o in range(2):
            for g in range(4):
                at = o * BLOCK + g * ACTF * H
                part = m_s[q % 2][at : at + ACTF * H, :] + b_in
                hb = part.astype(BF16)
                for f in range(2, ACTF):
                    h0_s[f - 2, o, 4 * g + q] = hb[f * H : (f + 1) * H]
                h = hb.astype(F32)
                scale = lax.rsqrt(jnp.mean(h * h, axis=-1, keepdims=True) + 1e-06)
                v = h * (scale * keep) * half_gain
                a = v + v * jnp.tanh(v)
                d = [a[f * H : (f + 1) * H] for f in range(ACTF)]
                for kt, r in enumerate(time_points(*d)):
                    lo, hi = r[:8], r[8:]
                    lo1, hi1 = pltpu.roll(lo, 1, 0), pltpu.roll(hi, 1, 0)
                    lo7, hi7 = pltpu.roll(lo, 7, 0), pltpu.roll(hi, 7, 0)
                    up = jnp.concatenate(
                        [jnp.where(sub == 0, 0.0, lo1), jnp.where(sub == 0, lo1, hi1)], axis=0
                    )
                    dn = jnp.concatenate(
                        [jnp.where(sub == 7, hi7, lo7), jnp.where(sub == 7, 0.0, hi7)], axis=0
                    )
                    at = vt[kt].at[1 - o, 4 * g + q + o]
                    at[:, :C] = up.astype(BF16)
                    at[:, C : 2 * C] = r.astype(BF16)
                    at[:, 2 * C :] = dn.astype(BF16)

    conv_in(0)
    for q in range(4):
        if q < 3:
            conv_in(q + 1)
        activate(q)
    copy_m.wait()

    def weights(kts, start, size):
        for dh in range(3):
            for i in range(start, start + size, 16):

                @functools.cache
                def tap(dt, dw):
                    at = ((dt * 3 + dh) * 3 + dw) * C + i
                    return wm[at : at + 16, :]

                for kt in kts:
                    g0, g1, g2 = (time_weights(kt, dw, tap) for dw in range(3))
                    e = g0 + g2
                    at = dh * C + i
                    for kc, u in enumerate((g0, e + g1, e - g1, g2)):
                        u_s[kt][kc, at : at + 16, :] = u

    def columns(n, j):
        kt = ORDER[n]
        for k in range(3):
            part = slice(k * C, (k + 1) * C)
            d0, d1 = vt[kt][0, j * 4, :, part], vt[kt][1, j * 4, :, part]
            for ct in range(j * 4, j * 4 + 4):
                d2, d3 = vt[kt][0, ct + 1, :, part], vt[kt][1, ct + 1, :, part]
                for kc, r in enumerate((d0 - d2, d1 + d2, d2 - d1, d1 - d3)):
                    v_s[n % 2][kc, ct * H : (ct + 1) * H, part] = r
                d0, d1 = d2, d3

    def product(n, kc):
        m_s[n % 2][kc * PAIRS * H : (kc + 1) * PAIRS * H, :] = jnp.dot(
            v_s[n % 2][kc], u_s[ORDER[n]][kc], preferred_element_type=F32
        )

    def inverse(n, ct):
        at = [(kc * PAIRS + ct) * H for kc in range(4)]
        m0, m1, m2, m3 = (m_s[n % 2][i : i + H, :] for i in at)
        return m0 + 0.5 * (m1 + m2), 0.5 * (m1 - m2) - m3

    def held(n, o, ct):
        at = ((n * 2 + o) * PAIRS + ct) * H
        return slice(at, at + H)

    weights((ORDER[0],), 0, C)
    for j in range(4):
        columns(0, j)

    for n in range(POINTS):
        for j in range(4):
            product(n, j)
            if n == 0:
                weights((ORDER[1],), j * QUARTER, QUARTER)
            if n < 2:
                weights(ORDER[2:4], (n * 4 + j) * EIGHTH, EIGHTH)
            elif n < 4:
                weights(ORDER[4:], (n * 4 + j - 8) * EIGHTH, EIGHTH)
            if n < POINTS - 1:
                columns(n + 1, j)
            if n > 0:
                for ct in range(j * 4, j * 4 + 4):
                    even, odd = inverse(n - 1, ct)
                    y_s[held(n - 1, 0, ct), :] = even
                    y_s[held(n - 1, 1, ct), :] = odd

    b_mid = bmid_ref[...].reshape(1, C)
    b_time = btime_ref[...].reshape(1, 2 * C)
    for ct in range(PAIRS):
        last = inverse(POINTS - 1, ct)
        for o in range(2):
            points = [y_s[held(n, o, ct), :] for n in range(POINTS - 1)] + [last[o]]
            points = [points[ORDER.index(kt)] for kt in range(POINTS)]
            for f, z in enumerate(time_frames(*points)):
                h1 = h0_s[f, o, ct].astype(F32) + (z + b_mid)
                if f < 2:
                    h1 = h1 * jnp.where(first - 2 + f >= 0, 1.0, 0.0).astype(F32)
                at = (o * PAIRS + ct) * H
                h1_s[f // 2][at : at + H, f % 2 * C : (f % 2 + 1) * C] = h1.astype(BF16)
    for t in range(2):
        hcat[:, 2 * t * C : 2 * (t + 1) * C] = jnp.dot(
            perm[...], h1_s[t][...], preferred_element_type=F32
        ).astype(BF16)
    copy_t.wait()
    sent = []
    for f in range(NT):
        for part in range(2):
            rows = slice(part * H * W // 2, (part + 1) * H * W // 2)
            up = jnp.dot(hcat[rows, f * C : f * C + K3], wt[...], preferred_element_type=F32) + b_time
            for s in range(2):
                u_s[0][2 * f + s, rows, :] = up[:, s * C : (s + 1) * C].astype(BF16)
            two = slice(2 * f, 2 * f + 2)
            copy = pltpu.make_async_copy(
                u_s[0].at[two, rows], out_hbm.at[two, rows], out_sems.at[f, part]
            )
            copy.start()
            sent.append(copy)
    for copy in sent:
        copy.wait()


def pack(latent_ref, out_ref, held):
    held[:LATF] = jnp.zeros_like(held[:LATF])
    held[LATF:] = latent_ref[...].astype(F32)
    for i in range(out_ref.shape[0]):
        out_ref[i] = held[NT * (i + 1) : NT * (i + 1) + LATF].astype(BF16)


def per_device(latent, w_in, b_in, gain, w_mid, b_mid, w_time, b_time):
    n = lax.axis_size("tm")
    frames, width = latent.shape
    sent = pl.pallas_call(
        pack,
        out_shape=jax.ShapeDtypeStruct((n, LATF, width), BF16),
        scratch_shapes=[pltpu.VMEM((LATF + frames, width), F32)],
    )(latent)
    x = lax.all_to_all(sent, "tm", split_axis=0, concat_axis=0, tiled=True)
    x = x.reshape(n * LATF, width)
    vmem = pl.BlockSpec(memory_space=pltpu.VMEM)
    hbm = pl.BlockSpec(memory_space=pl.ANY)
    out = pl.pallas_call(
        kernel,
        out_shape=jax.ShapeDtypeStruct((2 * NT, H * W, C), BF16),
        in_specs=[hbm, hbm, vmem, vmem, hbm, vmem, hbm, vmem],
        out_specs=hbm,
        scratch_shapes=[
            pltpu.VMEM((n * LATF, width), BF16),
            pltpu.VMEM((27 * ZC, C), BF16),
            pltpu.VMEM((27 * C, C), BF16),
            pltpu.VMEM((K3, 2 * C), BF16),
            pltpu.VMEM((2 * C, 2 * C), BF16),
            [pltpu.VMEM((BLOCK, 2 * C), BF16)] * 4,
            [pltpu.VMEM((H * W, 2 * C), BF16)] * 2,
            pltpu.VMEM((MIDF, 2, PAIRS, H, C), BF16),
            [pltpu.VMEM((2, PAIRS + 1, H, K3), BF16)] * POINTS,
            [pltpu.VMEM((4, PAIRS * H, K3), BF16)] * 2,
            [pltpu.VMEM((4, K3, C), BF16)] * POINTS,
            [pltpu.VMEM((4 * PAIRS * H, C), F32)] * 2,
            pltpu.VMEM(((POINTS - 1) * 2 * PAIRS * H, C), F32),
            pltpu.VMEM((H * W, MIDF * C), BF16),
            pltpu.VMEM((H * W, H * W), BF16),
            pltpu.SemaphoreType.DMA((4,)),
            pltpu.SemaphoreType.DMA((NT, 2)),
        ],
        compiler_params=pltpu.CompilerParams(vmem_limit_bytes=61 * 2**20),
    )(
        x, w_in.reshape(27 * ZC, C), b_in, gain, w_mid.reshape(27 * C, C), b_mid,
        w_time.reshape(K3, 2 * C), b_time,
    )
    return out.reshape(2 * NT, H, W, C)


def solution(mesh):
    return jax.shard_map(
        per_device,
        mesh=mesh,
        in_specs=(P("groups", "tm"), P(), P(), P(), P(), P(), P(), P()),
        out_specs=P(("groups", "tm"), None, None, None),
        check_vma=False,
    )
```
